32 devices in a mesh: groups: 2 (over y), blocks: 16 (over z, x, core).
Axes of the slice: x: 2, y: 2, z: 4, core: 2. Of those that a mesh axis runs over, the one named last changes fastest.
Arguments:
- snapshot: bfloat16 [2, 128, 32, 512], P('groups', 'blocks'), parts along dimension 0, may hold values from -6 to 6
- cotangent: bfloat16 [2, 128, 32, 512], P('groups', 'blocks'), parts along dimension 0, may hold values from -6 to 6
- first_weight: bfloat16 [32, 864], replicated, may hold values from -0.21875 to 0.21875
- second_weight: bfloat16 [32, 864], replicated, may hold values from -0.21875 to 0.21875
- face_codes: int32 [32, 2], P(('groups', 'blocks')), parts along dimension 0, may hold values from 0 to 3, as said below
Outputs:
- input_grad: float32 [2, 128, 32, 512], P('groups', 'blocks'), parts along dimension 0
- first_update: float32 [64, 864], P('groups'), parts along dimension 0
- second_update: float32 [64, 864], P('groups'), parts along dimension 0
The draws below stay inside these ranges and needn't reach their ends.
There are 2 independent parts, one for each index of `groups`. The reference program is written for one: setup_inputs(seed, part) draws one part's arguments, and reference() takes and returns one part's arrays. A program takes and returns all parts, laid end to end along the dimension named above; an argument that names none is the same for every part. Nothing has to cross between parts.
Inputs may be any that keep to these rules, and one draw needn't show every extreme that they name: face_codes[b, 1] equals face_codes[(b + 1) mod 16, 0]: both blocks of an interface carry the same code.
All inputs are finite; a program needn't handle non-finite values.
Results may differ from the reference program's by a relative error of at most 0.003.
Values may be sent and summed in bfloat16 or wider, within the bound.
A program may use at most 64 MiB of HBM per device.

```python
import jax
import jax.numpy as jnp
from jax import lax

CH = 32
TAPS = 27
R_CELLS = 32
Z_CELLS = 16
A_CELLS = 8
BATCH = 1
A_TOTAL = 128
RZ = 512
N_BLOCKS = 16


def draw_face_codes(key, part):
    codes = jax.random.randint(key, (N_BLOCKS,), 0, 4, dtype=jnp.int32)
    return jnp.stack([jnp.roll(codes, 1), codes], axis=1)


def block_levels(stream_key, shape, cuts, least, top_value):
    def one(position, blocks):
        steps = jax.random.uniform(jax.random.fold_in(jax.random.fold_in(stream_key, 6), position), (blocks,), jnp.float32, least / len(cuts), top_value / len(cuts))
        return jnp.repeat(jnp.exp(steps), shape[position] // blocks).reshape((-1,) + (1,) * (len(shape) - position - 1))

    level = one(*cuts[0])
    for cut in cuts[1:]:
        level = level * one(*cut)
    return level


def noise(stream_key, shape, scale, reach, shards=(), kind=jnp.bfloat16):
    gain = block_levels(stream_key, shape, shards, -0.22, 0.18) if shards else 1.0
    values = jax.random.normal(stream_key, shape, jnp.float32) * scale * gain
    return jnp.minimum(jnp.maximum(values, -reach), reach).astype(kind)


def setup_inputs(seed: int = 0, part: int = 0) -> dict:
    streams_of = jax.random.split(jax.random.key(seed), 6)
    part_keys = jax.random.split(jax.random.fold_in(streams_of[5], part), 6)
    return {
        "snapshot": noise(part_keys[0], (BATCH, A_TOTAL, CH, RZ), 1.0, 6.0, ((1, 16),)),
        "cotangent": noise(part_keys[1], (BATCH, A_TOTAL, CH, RZ), 1.0, 6.0, ((1, 16),)),
        "first_weight": noise(streams_of[2], (CH, TAPS * CH), (TAPS * CH) ** -0.5, 0.21875),
        "second_weight": noise(streams_of[3], (CH, TAPS * CH), (TAPS * CH) ** -0.5, 0.21875),
        "face_codes": draw_face_codes(jax.random.fold_in(jax.random.fold_in(streams_of[5], part), 71), part),
    }


def flip_planes(planes, codes):
    first_bit = (codes % 2 == 1)[None, :, None, None, None]
    planes = jnp.where(first_bit, planes[:, :, :, ::-1, :], planes)
    second_bit = (codes // 2 == 1)[None, :, None, None, None]
    return jnp.where(second_bit, planes[:, :, :, :, ::-1], planes)

def pad_domain(field, face_codes):
    lower = flip_planes(jnp.roll(field[:, :, -1], 1, axis=1), face_codes[:, 0])
    upper = flip_planes(jnp.roll(field[:, :, 0], -1, axis=1), face_codes[:, 1])
    full = jnp.concatenate([lower[:, :, None], field, upper[:, :, None]], axis=2)
    return jnp.pad(full, ((0, 0), (0, 0), (0, 0), (0, 0), (1, 1), (1, 1)))

def convolve(field, weight, face_codes):
    padded = pad_domain(field, face_codes)
    count = field.shape[2]
    channels = field.shape[3]
    radial = field.shape[4]
    vertical = field.shape[5]
    total = jnp.zeros(field.shape[:3] + (weight.shape[0], radial, vertical), jnp.float32)
    for step_a in range(3):
        for step_r in range(3):
            for step_z in range(3):
                tap_index = 9 * step_a + 3 * step_r + step_z
                piece = padded[:, :, step_a:step_a + count, :, step_r:step_r + radial, step_z:step_z + vertical]
                kernel = weight[:, tap_index * channels:(tap_index + 1) * channels]
                total = total + jnp.einsum('oc,bnacrz->bnaorz', kernel, piece)
    return total

def weight_gradient(field, cotan, face_codes):
    padded = pad_domain(field, face_codes)
    count = field.shape[2]
    radial = field.shape[4]
    vertical = field.shape[5]
    pieces = []
    for step_a in range(3):
        for step_r in range(3):
            for step_z in range(3):
                piece = padded[:, :, step_a:step_a + count, :, step_r:step_r + radial, step_z:step_z + vertical]
                pieces.append(jnp.einsum('bnaorz,bnacrz->oc', cotan, piece))
    return jnp.concatenate(pieces, axis=1)

def normalize(grad):
    return grad / jnp.sqrt(jnp.mean(grad * grad) + 1e-06)

def reference(snapshot, cotangent, first_weight, second_weight, face_codes):
    batch_count = snapshot.shape[0]
    shape_six = (batch_count, N_BLOCKS, A_CELLS, CH, R_CELLS, Z_CELLS)
    field = snapshot.astype(jnp.float32).reshape(shape_six)
    cotan = cotangent.astype(jnp.float32).reshape(shape_six)
    weight_one = first_weight.astype(jnp.float32)
    weight_two = second_weight.astype(jnp.float32)
    pre = convolve(field, weight_one, face_codes)
    hidden = lax.optimization_barrier(jax.nn.silu(pre).astype(jnp.bfloat16)).astype(jnp.float32)
    second_grad = weight_gradient(hidden, cotan, face_codes)
    _, back_two = jax.vjp(lambda value: convolve(value, weight_two, face_codes), hidden)
    hidden_grad, = back_two(cotan)
    sigmoid_part = jax.nn.sigmoid(pre)
    pre_grad = hidden_grad * sigmoid_part * (1.0 + pre * (1.0 - sigmoid_part))
    pre_grad = lax.optimization_barrier(pre_grad.astype(jnp.bfloat16)).astype(jnp.float32)
    first_grad = weight_gradient(field, pre_grad, face_codes)
    _, back_one = jax.vjp(lambda value: convolve(value, weight_one, face_codes), field)
    field_grad, = back_one(pre_grad)
    input_grad = (cotan + field_grad).reshape(batch_count, N_BLOCKS * A_CELLS, CH, R_CELLS * Z_CELLS)
    return (input_grad, normalize(first_grad), normalize(second_grad))
```

```python
import functools

import jax
import jax.numpy as jnp
from jax import lax
from jax.experimental import pallas as pl
from jax.experimental.pallas import tpu as pltpu
from jax.sharding import PartitionSpec as P

R_CELLS = 32
CH = 32
PLANES = 8
LANES = 384
MAIN = 256
PIECES = 14
PIECE = 16
MESH = pl.DeviceIdType.MESH
POSITIONS = [0, 1, 2, 3, 4, 5, 6, 7, -2, -1, 8, 9]
F32 = jnp.float32
BF16 = jnp.bfloat16


def lane_place(position):
    index = POSITIONS.index(position)
    return index // 4, index % 4


def kernel(
    n, vertical,
    snap_ref, cot_ref, w1_ref, w2_ref, codes_ref,
    out_ref, up1_ref, up2_ref,
    halo, taps, ops1, ops2, xs, cs, hs, ps, slope, pg_nat, g1, g2, rs1, rs2, own1, own2, ag1, ag2,
    halo_send, halo_recv,
    rs1_send, rs1_recv, rs2_send, rs2_recv, ag1_send, ag1_recv, ag2_send, ag2_recv,
):
    cells = snap_ref.shape[1]
    wide = cells + 2 * vertical
    me = lax.axis_index("blocks")
    after, before = lax.rem(me + 1, n), lax.rem(me + n - 1, n)

    barrier = pltpu.get_barrier_semaphore()

    def greet(k, carry):
        pl.semaphore_signal(
            barrier, inc=1, device_id={"blocks": lax.rem(me + k, n)}, device_id_type=MESH
        )
        return carry

    lax.fori_loop(1, n, greet, 0)

    lane128 = lax.broadcasted_iota(jnp.int32, (CH, 128), 1)
    lane_block = lane128 // CH
    low, high = codes_ref[0, 0], codes_ref[0, 1]
    code_lane = jnp.where(lane_block < 2, low, high)
    flip_r = (code_lane % 2) == 1
    flip_z = (code_lane // 2) == 1

    pl.semaphore_wait(barrier, n - 1)

    copies = []
    for index, (source, rows, target, side) in enumerate([
        (snap_ref, 6 * CH, after, 0),
        (snap_ref, 0, before, 1),
        (cot_ref, 6 * CH, after, 0),
        (cot_ref, 0, before, 1),
    ]):
        copy = pltpu.make_async_remote_copy(
            src_ref=source.at[pl.ds(rows, 2 * CH)],
            dst_ref=halo.at[side, pl.ds((index // 2) * 2 * CH, 2 * CH)],
            send_sem=halo_send.at[index],
            recv_sem=halo_recv.at[index],
            device_id={"blocks": target},
            device_id_type=MESH,
        )
        copy.start()
        copies.append(copy)

    spread = (
        lax.broadcasted_iota(jnp.int32, (CH, 128), 0) == lane128 % CH
    ).astype(F32).astype(BF16)

    def build(weight_ref, ops):
        taps[...] = lax.dot_general(
            weight_ref[...], spread, (((0,), (0,)), ((), ())), preferred_element_type=F32
        )

        def tap_step(tau, carry):
            dr, dz = tau // 3, tau % 3

            def tap(da, r, z):
                start = pl.multiple_of((9 * da + 3 * r + z) * CH, CH)
                return taps[pl.ds(start, CH), :]

            plain = [tap(da, dr, dz) for da in range(3)]
            turned = [
                jnp.where(
                    flip_r,
                    jnp.where(flip_z, tap(da, 2 - dr, 2 - dz), tap(da, 2 - dr, dz)),
                    jnp.where(flip_z, tap(da, dr, 2 - dz), plain[da]),
                )
                for da in range(3)
            ]
            for x, position in enumerate(POSITIONS):
                for tile in range(3):
                    value = jnp.zeros((CH, 128), F32)
                    for da in range(3):
                        wanted = position - da + 1
                        if wanted < -2 or wanted > 9:
                            continue
                        place = lane_place(wanted)
                        if place[0] != tile:
                            continue
                        source = turned[da] if tile == 2 else plain[da]
                        value = jnp.where(lane_block == place[1], source, value)
                    ops[tau, pl.ds(x * CH, CH), pl.ds(tile * 128, 128)] = value.astype(BF16)
            return carry

        lax.fori_loop(0, 9, tap_step, 0)

    def put(dst, start, first_lane, value):
        rows, lanes = value.shape
        z = lax.broadcasted_iota(jnp.int32, (rows, lanes), 0) % vertical
        moved = [
            jnp.where(z == 0, 0.0, pltpu.roll(value, 1, 0)),
            value,
            jnp.where(z == vertical - 1, 0.0, pltpu.roll(value, rows - 1, 0)),
        ]
        for dz in range(3):
            dst[dz, pl.ds(start, rows), pl.ds(first_lane, lanes)] = moved[dz].astype(BF16)

    edge = jnp.zeros((3, vertical, LANES), BF16)
    for field in (xs, cs, hs, ps):
        field[:, pl.ds(0, vertical), :] = edge
        field[:, pl.ds(wide - vertical, vertical), :] = edge

    put(xs, vertical, 0, snap_ref[...].astype(F32).T)
    put(cs, vertical, 0, cot_ref[...].astype(F32).T)
    build(w1_ref, ops1)
    build(w2_ref, ops2)

    row_cell = lax.broadcasted_iota(jnp.int32, (cells, cells), 0)
    column_cell = lax.broadcasted_iota(jnp.int32, (cells, cells), 1)
    radial_bits = cells - vertical
    swaps = []
    for code in (low, high):
        mask = (code % 2) * radial_bits + (code // 2) * (vertical - 1)
        swaps.append((row_cell == jnp.bitwise_xor(column_cell, mask)).astype(F32).astype(BF16))

    for copy in copies:
        copy.wait()

    sides = [
        jnp.dot(halo[side], swaps[side], preferred_element_type=F32) for side in range(2)
    ]
    put(xs, vertical, MAIN, jnp.concatenate([sides[0][: 2 * CH], sides[1][: 2 * CH]], axis=0).T)
    put(cs, vertical, MAIN, jnp.concatenate([sides[0][2 * CH :], sides[1][2 * CH :]], axis=0).T)

    chunk = 256

    def forward(field, ops, start):
        total = None
        for dr in range(3):
            for dz in range(3):
                term = jnp.dot(
                    field[dz, pl.ds(start + dr * vertical, chunk), :],
                    ops[3 * dr + dz],
                    preferred_element_type=F32,
                )
                total = term if total is None else total + term
        return total

    def backward(field, ops, start, outs):
        total = None
        for dr in range(3):
            for dz in range(3):
                term = lax.dot_general(
                    field[2 - dz, pl.ds(start + (2 - dr) * vertical, chunk), :],
                    ops[3 * dr + dz, pl.ds(0, outs), :],
                    (((1,), (1,)), ((), ())),
                    preferred_element_type=F32,
                )
                total = term if total is None else total + term
        return total

    def gradient(left, field, result):
        lane = lax.broadcasted_iota(jnp.int32, (CH, 128), 1) // CH
        found = {}
        for dr in range(3):
            for dz in range(3):
                full = jnp.dot(
                    left[...],
                    field[dz, pl.ds(dr * vertical, cells), :],
                    preferred_element_type=F32,
                )
                for da in range(3):
                    total = None
                    for a in range(PLANES):
                        tile, block = lane_place(a + da - 1)
                        piece = full[a * CH : (a + 1) * CH, tile * 128 : (tile + 1) * 128]
                        term = jnp.where(lane == block, piece, 0.0)
                        total = term if total is None else total + term
                    total = total + pltpu.roll(total, 64, 1)
                    total = total + pltpu.roll(total, 32, 1)
                    found[9 * da + 3 * dr + dz] = total
        for tile in range(7):
            value = jnp.zeros((CH, 128), F32)
            for block in range(4):
                if 4 * tile + block < 27:
                    value = jnp.where(lane == block, found[4 * tile + block], value)
            result[pl.ds(tile * CH, CH), :] = value

    def scatter_copy(grad, slots, send, recv, owner, source):
        return pltpu.make_async_remote_copy(
            src_ref=grad.at[pl.ds(pl.multiple_of(owner * PIECE, PIECE), PIECE)],
            dst_ref=slots.at[source],
            send_sem=send.at[owner],
            recv_sem=recv.at[source],
            device_id={"blocks": owner},
            device_id_type=MESH,
        )

    def scatter_start(grad, slots, send, recv):
        def one(k, carry):
            owner = lax.rem(me + k, n)

            @pl.when(owner < PIECES)
            def _():
                scatter_copy(grad, slots, send, recv, owner, me).start()

            return carry

        lax.fori_loop(1, n, one, 0)

        @pl.when(me < PIECES)
        def _():
            slots[me] = grad[pl.ds(pl.multiple_of(me * PIECE, PIECE), PIECE), :]

    def gather_copy(own, gathered, send, recv, owner, target):
        return pltpu.make_async_remote_copy(
            src_ref=own,
            dst_ref=gathered.at[owner],
            send_sem=send.at[target],
            recv_sem=recv.at[owner],
            device_id={"blocks": target},
            device_id_type=MESH,
        )

    def reduce_and_gather(grad, slots, send, recv, own, gathered, gsend, grecv):
        @pl.when(me < PIECES)
        def _():
            def one(k, carry):
                source = lax.rem(me + k, n)
                scatter_copy(grad, slots, send, recv, me, source).wait_recv()
                return carry

            lax.fori_loop(1, n, one, 0)
            total = jnp.sum(slots[...], axis=0).astype(BF16)
            own[...] = total
            gathered[me] = total

            def out(k, carry):
                gather_copy(own, gathered, gsend, grecv, me, lax.rem(me + k, n)).start()
                return carry

            lax.fori_loop(1, n, out, 0)

    def finish(grad, slots, send, recv, own, gathered, gsend, grecv, up_ref):
        def sent(k, carry):
            owner = lax.rem(me + k, n)

            @pl.when(owner < PIECES)
            def _():
                scatter_copy(grad, slots, send, recv, owner, me).wait_send()
                gather_copy(own, gathered, gsend, grecv, owner, me).wait_recv()

            return carry

        lax.fori_loop(1, n, sent, 0)
        value = gathered[...].astype(F32).reshape(PIECES * PIECE, 128)
        scale = lax.rsqrt(jnp.sum(value * value) / (CH * 27 * CH) + 1e-06)
        value = value * scale
        for tile in range(7):
            lanes = 128 if tile < 6 else 96
            up_ref[:, pl.ds(tile * 128, lanes)] = value[tile * CH : (tile + 1) * CH, :lanes]

        @pl.when(me < PIECES)
        def _():
            def out(k, carry):
                gather_copy(own, gathered, gsend, grecv, me, lax.rem(me + k, n)).wait_send()
                return carry

            lax.fori_loop(1, n, out, 0)

    set1 = (g1, rs1, rs1_send, rs1_recv, own1, ag1, ag1_send, ag1_recv)
    set2 = (g2, rs2, rs2_send, rs2_recv, own2, ag2, ag2_send, ag2_recv)

    for start in range(0, cells, chunk):
        pre = forward(xs, ops1, start)
        s = 1.0 / (1.0 + jnp.exp(-pre))
        hidden = (pre * s).astype(BF16)
        slope[pl.ds(start, chunk), :] = s * (1.0 + pre * (1.0 - s))
        put(hs, start + vertical, 0, hidden.astype(F32))

    gradient(cot_ref, hs, g2)
    scatter_start(*set2[:4])

    for start in range(0, cells, chunk):
        back = backward(cs, ops2, start, LANES)
        value = (back * slope[pl.ds(start, chunk), :]).astype(BF16).astype(F32)
        put(ps, start + vertical, 0, value)
        pg_nat[:, pl.ds(start, chunk)] = value[:, :MAIN].T.astype(BF16)

    gradient(pg_nat, xs, g1)
    scatter_start(*set1[:4])
    reduce_and_gather(*set2)

    for start in range(0, cells, chunk):
        back = backward(ps, ops1, start, MAIN)
        out_ref[:, pl.ds(start, chunk)] = back.T + cot_ref[:, pl.ds(start, chunk)].astype(F32)

    reduce_and_gather(*set1)
    finish(*set2, up2_ref)
    finish(*set1, up1_ref)


def solution(mesh):
    n = mesh.shape["blocks"]

    def body(snapshot, cotangent, first_weight, second_weight, face_codes):
        cells = snapshot.shape[3]
        vertical = cells // R_CELLS
        wide = cells + 2 * vertical
        flat = (PLANES * CH, cells)
        vmem = pl.BlockSpec(memory_space=pltpu.VMEM)
        dma = pltpu.SemaphoreType.DMA
        grad, up1, up2 = pl.pallas_call(
            functools.partial(kernel, n, vertical),
            out_shape=(
                jax.ShapeDtypeStruct(flat, F32),
                jax.ShapeDtypeStruct(first_weight.shape, F32),
                jax.ShapeDtypeStruct(second_weight.shape, F32),
            ),
            in_specs=[vmem] * 4 + [pl.BlockSpec(memory_space=pltpu.SMEM)],
            out_specs=(vmem, vmem, vmem),
            scratch_shapes=[
                pltpu.VMEM((2, 4 * CH, cells), BF16),
                pltpu.VMEM((27 * CH, 128), F32),
                pltpu.VMEM((9, LANES, LANES), BF16),
                pltpu.VMEM((9, LANES, LANES), BF16),
                pltpu.VMEM((3, wide, LANES), BF16),
                pltpu.VMEM((3, wide, LANES), BF16),
                pltpu.VMEM((3, wide, LANES), BF16),
                pltpu.VMEM((3, wide, LANES), BF16),
                pltpu.VMEM((cells, LANES), F32),
                pltpu.VMEM(flat, BF16),
                pltpu.VMEM((PIECES * PIECE, 128), F32),
                pltpu.VMEM((PIECES * PIECE, 128), F32),
                pltpu.VMEM((n, PIECE, 128), F32),
                pltpu.VMEM((n, PIECE, 128), F32),
                pltpu.VMEM((PIECE, 128), BF16),
                pltpu.VMEM((PIECE, 128), BF16),
                pltpu.VMEM((PIECES, PIECE, 128), BF16),
                pltpu.VMEM((PIECES, PIECE, 128), BF16),
                dma((4,)),
                dma((4,)),
                dma((PIECES,)),
                dma((n,)),
                dma((PIECES,)),
                dma((n,)),
                dma((n,)),
                dma((PIECES,)),
                dma((n,)),
                dma((PIECES,)),
            ],
            compiler_params=pltpu.CompilerParams(
                collective_id=0, has_side_effects=True, vmem_limit_bytes=48 * 1024 * 1024
            ),
        )(
            snapshot.reshape(flat),
            cotangent.reshape(flat),
            first_weight,
            second_weight,
            face_codes,
        )
        return grad.reshape(snapshot.shape), up1, up2

    return jax.shard_map(
        body,
        mesh=mesh,
        in_specs=(
            P("groups", "blocks", None, None),
            P("groups", "blocks", None, None),
            P(),
            P(),
            P(("groups", "blocks"), None),
        ),
        out_specs=(P("groups", "blocks", None, None), P("groups", None), P("groups", None)),
        check_vma=False,
    )
```

```python
import functools

import jax
import jax.numpy as jnp
from jax import lax
from jax.experimental import pallas as pl
from jax.experimental.pallas import tpu as pltpu
from jax.sharding import PartitionSpec as P

R_CELLS = 32
CH = 32
PLANES = 8
LANES = 384
MAIN = 256
PIECES = 14
PIECE = 16
MESH = pl.DeviceIdType.MESH
POSITIONS = [0, 1, 2, 3, 4, 5, 6, 7, -2, -1, 8, 9]
F32 = jnp.float32
BF16 = jnp.bfloat16


def lane_place(position):
    index = POSITIONS.index(position)
    return index // 4, index % 4


HALO = [-2, -1, 8, 9]
INNER = list(range(PLANES))


def kernel(
    n, vertical,
    snap_in, cot_in, w1_in, w2_in, codes_in,
    out_ref, up1_ref, up2_ref,
    snap_ref, cot_ref, w1_ref, w2_ref, codes_ref,
    halo, taps, main1, main2, side1, side2, back1, edge1, edge2,
    xs, xh, xe, cs, ch, ce, hs, hh, ps, ph,
    pg_nat, cot_edge, g1, g2, rs1, rs2, own1, own2, ag1, ag2,
    load_sem, halo_send, halo_recv,
    rs1_send, rs1_recv, rs2_send, rs2_recv, ag1_send, ag1_recv, ag2_send, ag2_recv,
):
    cells = snap_ref.shape[1]
    wide = cells + 2 * vertical
    me = lax.axis_index("blocks")
    after, before = lax.rem(me + 1, n), lax.rem(me + n - 1, n)

    barrier = pltpu.get_barrier_semaphore()

    def greet(k, carry):
        pl.semaphore_signal(
            barrier, inc=1, device_id={"blocks": lax.rem(me + k, n)}, device_id_type=MESH
        )
        return carry

    lax.fori_loop(1, n, greet, 0)

    loads = [
        pltpu.make_async_copy(source, target, load_sem.at[index])
        for index, (source, target) in enumerate([
            (codes_in, codes_ref), (w1_in, w1_ref), (w2_in, w2_ref), (snap_in, snap_ref), (cot_in, cot_ref)
        ])
    ]
    for load in loads:
        load.start()

    for field in (xs, cs, hs, ps):
        field[:, pl.ds(0, vertical), :] = jnp.zeros((3, vertical, MAIN), BF16)
        field[:, pl.ds(wide - vertical, vertical), :] = jnp.zeros((3, vertical, MAIN), BF16)
    for field in (xh, ch, hh, ph, xe, ce):
        field[pl.ds(0, vertical), :] = jnp.zeros((vertical, field.shape[1]), BF16)
        field[pl.ds(wide - vertical, vertical), :] = jnp.zeros((vertical, field.shape[1]), BF16)

    pl.semaphore_wait(barrier, n - 1)

    copies = []
    for index, (source, rows, target, side) in enumerate([
        (snap_in, 6 * CH, after, 0),
        (snap_in, 0, before, 1),
        (cot_in, 6 * CH, after, 0),
        (cot_in, 0, before, 1),
    ]):
        copy = pltpu.make_async_remote_copy(
            src_ref=source.at[pl.ds(rows, 2 * CH)],
            dst_ref=halo.at[side, pl.ds((index // 2) * 2 * CH, 2 * CH)],
            send_sem=halo_send.at[index],
            recv_sem=halo_recv.at[index],
            device_id={"blocks": target},
            device_id_type=MESH,
        )
        copy.start()
        copies.append(copy)

    for load in loads:
        load.wait()

    lane_block = lax.broadcasted_iota(jnp.int32, (CH, 128), 1) // CH
    low, high = codes_ref[0, 0], codes_ref[0, 1]
    code_lane = jnp.where(lane_block < 2, low, high)
    flip_r = (code_lane % 2) == 1
    flip_z = (code_lane // 2) == 1
    spread = (
        lax.broadcasted_iota(jnp.int32, (CH, 128), 0)
        == lax.broadcasted_iota(jnp.int32, (CH, 128), 1) % CH
    ).astype(F32).astype(BF16)

    def tap(da, r, z):
        start = pl.multiple_of((9 * da + 3 * r + z) * CH, CH)
        return taps[pl.ds(start, CH), :]

    def turned(da, r, z):
        return jnp.where(
            flip_r,
            jnp.where(flip_z, tap(da, 2 - r, 2 - z), tap(da, 2 - r, z)),
            jnp.where(flip_z, tap(da, r, 2 - z), tap(da, r, z)),
        )

    def block(x, columns, dr):
        value = jnp.zeros((CH, 128), F32)
        for index, column in enumerate(columns):
            if column is None:
                continue
            y, dz = column
            da = x - y + 1
            if 0 <= da <= 2:
                source = turned(da, dr, dz) if y in HALO else tap(da, dr, dz)
                value = jnp.where(lane_block == index, source, value)
        return value.astype(BF16)

    def plane_tiles(dz):
        return [[(y, dz) for y in group] for group in (INNER[:4], INNER[4:], HALO)]

    def spread_taps(weight_ref):
        taps[...] = lax.dot_general(
            weight_ref[...], spread, (((0,), (0,)), ((), ())), preferred_element_type=F32
        )

    def fill(ref, lead, row, tile, value):
        ref[lead, pl.ds(row * CH, CH), pl.ds(tile * 128, 128)] = value

    def build_main(dr, main):
        for dz in range(3):
            for row, x in enumerate(INNER):
                for tile in range(2):
                    fill(main, 3 * dr + dz, row, tile, block(x, plane_tiles(dz)[tile], dr))

    def build_forward(dr, side, edge):
        row = 0
        for dz in range(3):
            for x in HALO:
                for tile in range(3):
                    fill(side, dr, row, tile, block(x, plane_tiles(dz)[tile], dr))
                row += 1
        row = 0
        for dz in range(3):
            for x in (0, 7):
                fill(edge, dr, row, 0, block(x, plane_tiles(dz)[2], dr))
                row += 1
        for row in (6, 7):
            fill(edge, dr, row, 0, jnp.zeros((CH, 128), BF16))

    def build_backward(dr, side, edge, planes):
        for row, x in enumerate(planes):
            for moved in range(3):
                fill(side, dr, row, moved, block(x, plane_tiles(2 - moved)[2], dr))
        if edge is not None:
            for row, x in enumerate(HALO):
                fill(edge, dr, row, 0, block(x, [(0, 2), (7, 2), (0, 1), (7, 1)], dr))
                fill(edge, dr, row, 1, block(x, [(0, 0), (7, 0), None, None], dr))

    def shifts(value):
        rows, lanes = value.shape
        z = lax.broadcasted_iota(jnp.int32, (rows, lanes), 0) % vertical
        return [
            jnp.where(z == 0, 0.0, pltpu.roll(value, 1, 0)),
            value,
            jnp.where(z == vertical - 1, 0.0, pltpu.roll(value, rows - 1, 0)),
        ]

    inside = pl.ds(vertical, cells)

    def put_main(dst, value):
        for dz, moved in enumerate(shifts(value)):
            dst[dz, inside, :] = moved.astype(BF16)

    def put_halo(dst, value):
        for dz, moved in enumerate(shifts(value)):
            dst[inside, pl.ds(dz * 128, 128)] = moved.astype(BF16)

    def put_edge(dst, source):
        ends = jnp.concatenate([source[:CH, :], source[7 * CH :, :]] * 2, axis=0)
        moved = shifts(ends.astype(F32).T)
        first = lax.broadcasted_iota(jnp.int32, (cells, 128), 1) < 64
        dst[inside, pl.ds(0, 128)] = jnp.where(first, moved[0], moved[1]).astype(BF16)
        dst[inside, pl.ds(128, 128)] = jnp.where(first, moved[2], 0.0).astype(BF16)

    put_main(xs, snap_ref[...].astype(F32).T)
    put_edge(xe, snap_ref)
    spread_taps(w1_ref)

    def build1(dr, carry):
        build_main(dr, main1)
        build_forward(dr, side1, edge1)
        build_backward(dr, back1, None, INNER)
        return carry

    lax.fori_loop(0, 3, build1, 0)
    put_main(cs, cot_ref[...].astype(F32).T)
    put_edge(ce, cot_ref)
    cot_edge[pl.ds(0, CH), :] = cot_ref[pl.ds(0, CH), :]
    cot_edge[pl.ds(CH, CH), :] = cot_ref[pl.ds(7 * CH, CH), :]
    spread_taps(w2_ref)

    def build2(dr, carry):
        build_main(dr, main2)
        build_backward(dr, side2, edge2, INNER + HALO)
        return carry

    lax.fori_loop(0, 3, build2, 0)

    row_cell = lax.broadcasted_iota(jnp.int32, (cells, cells), 0)
    column_cell = lax.broadcasted_iota(jnp.int32, (cells, cells), 1)
    radial_bits = cells - vertical
    swaps = []
    for code in (low, high):
        mask = (code % 2) * radial_bits + (code // 2) * (vertical - 1)
        swaps.append((row_cell == jnp.bitwise_xor(column_cell, mask)).astype(F32).astype(BF16))

    for copy in copies:
        copy.wait()

    sides = [
        jnp.dot(halo[side], swaps[side], preferred_element_type=F32) for side in range(2)
    ]
    put_halo(xh, jnp.concatenate([sides[0][: 2 * CH], sides[1][: 2 * CH]], axis=0).T)
    put_halo(ch, jnp.concatenate([sides[0][2 * CH :], sides[1][2 * CH :]], axis=0).T)

    def added(total, term):
        return term if total is None else total + term

    def nn(left, right):
        return jnp.dot(left, right, preferred_element_type=F32)

    def nt(left, right):
        return lax.dot_general(left, right, (((1,), (1,)), ((), ())), preferred_element_type=F32)

    def up(step_r):
        return pl.ds(step_r * vertical, cells)

    def forward():
        inner, outer = None, None
        for dr in range(3):
            for dz in range(3):
                inner = added(inner, nn(xs[dz, up(dr), :], main1[3 * dr + dz]))
            inner = added(inner, nn(xh[up(dr), :], side1[dr, :, :MAIN]))
            outer = added(outer, nn(xh[up(dr), :], side1[dr, :, MAIN:]))
            outer = added(outer, nn(xe[up(dr), :], edge1[dr]))
        return inner, outer

    def backward(field, halos, main, side):
        inner = None
        for dr in range(3):
            for dz in range(3):
                inner = added(inner, nt(field[2 - dz, up(2 - dr), :], main[3 * dr + dz]))
            inner = added(inner, nt(halos[up(2 - dr), :], side[dr, :MAIN, :]))
        return inner

    def backward_outer(halos, ends, side, edge):
        outer = None
        for dr in range(3):
            outer = added(outer, nt(halos[up(2 - dr), :], side[dr, MAIN:, :]))
            outer = added(outer, nt(ends[up(2 - dr), :], edge[dr]))
        return outer

    def gradient(left, ends, field, halos, result):
        found = {}
        for dr in range(3):
            outer = nn(ends, halos[up(dr), :])
            for dz in range(3):
                full = nn(left, field[dz, up(dr), :])
                for da in range(3):
                    total = None
                    for a in range(PLANES):
                        tile, place = lane_place(a + da - 1)
                        if tile == 2:
                            row = 0 if a == 0 else CH
                            piece = outer[row : row + CH, dz * 128 : (dz + 1) * 128]
                        else:
                            piece = full[a * CH : (a + 1) * CH, tile * 128 : (tile + 1) * 128]
                        total = added(total, jnp.where(lane_block == place, piece, 0.0))
                    total = total + pltpu.roll(total, 64, 1)
                    total = total + pltpu.roll(total, 32, 1)
                    found[9 * da + 3 * dr + dz] = total
        for tile in range(7):
            value = jnp.zeros((CH, 128), F32)
            for place in range(4):
                if 4 * tile + place < 27:
                    value = jnp.where(lane_block == place, found[4 * tile + place], value)
            result[pl.ds(tile * CH, CH), :] = value

    def scatter_copy(grad, slots, send, recv, owner, source):
        return pltpu.make_async_remote_copy(
            src_ref=grad.at[pl.ds(pl.multiple_of(owner * PIECE, PIECE), PIECE)],
            dst_ref=slots.at[source],
            send_sem=send.at[owner],
            recv_sem=recv.at[source],
            device_id={"blocks": owner},
            device_id_type=MESH,
        )

    def scatter_start(grad, slots, send, recv):
        def one(k, carry):
            owner = lax.rem(me + k, n)

            @pl.when(owner < PIECES)
            def _():
                scatter_copy(grad, slots, send, recv, owner, me).start()

            return carry

        lax.fori_loop(1, n, one, 0)

        @pl.when(me < PIECES)
        def _():
            slots[me] = grad[pl.ds(pl.multiple_of(me * PIECE, PIECE), PIECE), :]

    def gather_copy(own, gathered, send, recv, owner, target):
        return pltpu.make_async_remote_copy(
            src_ref=own,
            dst_ref=gathered.at[owner],
            send_sem=send.at[target],
            recv_sem=recv.at[owner],
            device_id={"blocks": target},
            device_id_type=MESH,
        )

    def reduce_and_gather(grad, slots, send, recv, own, gathered, gsend, grecv):
        @pl.when(me < PIECES)
        def _():
            def one(k, carry):
                source = lax.rem(me + k, n)
                scatter_copy(grad, slots, send, recv, me, source).wait_recv()
                return carry

            lax.fori_loop(1, n, one, 0)
            total = jnp.sum(slots[...], axis=0).astype(BF16)
            own[...] = total
            gathered[me] = total

            def out(k, carry):
                gather_copy(own, gathered, gsend, grecv, me, lax.rem(me + k, n)).start()
                return carry

            lax.fori_loop(1, n, out, 0)

    def finish(grad, slots, send, recv, own, gathered, gsend, grecv, up_ref):
        def sent(k, carry):
            owner = lax.rem(me + k, n)

            @pl.when(owner < PIECES)
            def _():
                scatter_copy(grad, slots, send, recv, owner, me).wait_send()
                gather_copy(own, gathered, gsend, grecv, owner, me).wait_recv()

            return carry

        lax.fori_loop(1, n, sent, 0)
        value = gathered[...].astype(F32).reshape(PIECES * PIECE, 128)
        scale = lax.rsqrt(jnp.sum(value * value) / (CH * 27 * CH) + 1e-06)
        value = value * scale
        for tile in range(7):
            lanes = 128 if tile < 6 else 96
            up_ref[:, pl.ds(tile * 128, lanes)] = value[tile * CH : (tile + 1) * CH, :lanes]

        @pl.when(me < PIECES)
        def _():
            def out(k, carry):
                gather_copy(own, gathered, gsend, grecv, me, lax.rem(me + k, n)).wait_send()
                return carry

            lax.fori_loop(1, n, out, 0)

    set1 = (g1, rs1, rs1_send, rs1_recv, own1, ag1, ag1_send, ag1_recv)
    set2 = (g2, rs2, rs2_send, rs2_recv, own2, ag2, ag2_send, ag2_recv)

    def activate(pre):
        s = 1.0 / (1.0 + jnp.exp(-pre))
        return (pre * s).astype(BF16).astype(F32), s * (1.0 + pre * (1.0 - s))

    inner, outer = forward()
    hidden, slope = activate(inner)
    hidden_outer, slope_outer = activate(outer)
    put_main(hs, hidden)
    put_halo(hh, hidden_outer)

    gradient(cot_ref[...], cot_edge[...], hs, hh, g2)
    scatter_start(*set2[:4])

    value = (backward(cs, ch, main2, side2) * slope).astype(BF16).astype(F32)
    put_main(ps, value)
    pg_nat[...] = value.T.astype(BF16)
    value = (backward_outer(ch, ce, side2, edge2) * slope_outer).astype(BF16).astype(F32)
    put_halo(ph, value)

    ends = jnp.concatenate([pg_nat[:CH, :], pg_nat[7 * CH :, :]], axis=0)
    gradient(pg_nat[...], ends, xs, xh, g1)
    scatter_start(*set1[:4])
    reduce_and_gather(*set2)

    out_ref[...] = backward(ps, ph, main1, back1).T + cot_ref[...].astype(F32)

    reduce_and_gather(*set1)
    finish(*set2, up2_ref)
    finish(*set1, up1_ref)


def solution(mesh):
    n = mesh.shape["blocks"]

    def body(snapshot, cotangent, first_weight, second_weight, face_codes):
        cells = snapshot.shape[3]
        vertical = cells // R_CELLS
        wide = cells + 2 * vertical
        flat = (PLANES * CH, cells)
        vmem = pl.BlockSpec(memory_space=pltpu.VMEM)
        dma = pltpu.SemaphoreType.DMA
        grad, up1, up2 = pl.pallas_call(
            functools.partial(kernel, n, vertical),
            out_shape=(
                jax.ShapeDtypeStruct(flat, F32),
                jax.ShapeDtypeStruct(first_weight.shape, F32),
                jax.ShapeDtypeStruct(second_weight.shape, F32),
            ),
            in_specs=[pl.BlockSpec(memory_space=pltpu.HBM)] * 5,
            out_specs=(vmem, vmem, vmem),
            scratch_shapes=[
                pltpu.VMEM(flat, BF16),
                pltpu.VMEM(flat, BF16),
                pltpu.VMEM(first_weight.shape, BF16),
                pltpu.VMEM(second_weight.shape, BF16),
                pltpu.SMEM((1, 2), jnp.int32),
                pltpu.VMEM((2, 4 * CH, cells), BF16),
                pltpu.VMEM((27 * CH, 128), F32),
                pltpu.VMEM((9, MAIN, MAIN), BF16),
                pltpu.VMEM((9, MAIN, MAIN), BF16),
                pltpu.VMEM((3, LANES, LANES), BF16),
                pltpu.VMEM((3, LANES, LANES), BF16),
                pltpu.VMEM((3, MAIN, LANES), BF16),
                pltpu.VMEM((3, MAIN, 128), BF16),
                pltpu.VMEM((3, 128, MAIN), BF16),
                pltpu.VMEM((3, wide, MAIN), BF16),
                pltpu.VMEM((wide, LANES), BF16),
                pltpu.VMEM((wide, MAIN), BF16),
                pltpu.VMEM((3, wide, MAIN), BF16),
                pltpu.VMEM((wide, LANES), BF16),
                pltpu.VMEM((wide, MAIN), BF16),
                pltpu.VMEM((3, wide, MAIN), BF16),
                pltpu.VMEM((wide, LANES), BF16),
                pltpu.VMEM((3, wide, MAIN), BF16),
                pltpu.VMEM((wide, LANES), BF16),
                pltpu.VMEM(flat, BF16),
                pltpu.VMEM((2 * CH, cells), BF16),
                pltpu.VMEM((PIECES * PIECE, 128), F32),
                pltpu.VMEM((PIECES * PIECE, 128), F32),
                pltpu.VMEM((n, PIECE, 128), F32),
                pltpu.VMEM((n, PIECE, 128), F32),
                pltpu.VMEM((PIECE, 128), BF16),
                pltpu.VMEM((PIECE, 128), BF16),
                pltpu.VMEM((PIECES, PIECE, 128), BF16),
                pltpu.VMEM((PIECES, PIECE, 128), BF16),
                dma((5,)),
                dma((4,)),
                dma((4,)),
                dma((PIECES,)),
                dma((n,)),
                dma((PIECES,)),
                dma((n,)),
                dma((n,)),
                dma((PIECES,)),
                dma((n,)),
                dma((PIECES,)),
            ],
            compiler_params=pltpu.CompilerParams(
                collective_id=0, has_side_effects=True, vmem_limit_bytes=48 * 1024 * 1024
            ),
        )(
            snapshot.reshape(flat),
            cotangent.reshape(flat),
            first_weight,
            second_weight,
            face_codes,
        )
        return grad.reshape(snapshot.shape), up1, up2

    return jax.shard_map(
        body,
        mesh=mesh,
        in_specs=(
            P("groups", "blocks", None, None),
            P("groups", "blocks", None, None),
            P(),
            P(),
            P(("groups", "blocks"), None),
        ),
        out_specs=(P("groups", "blocks", None, None), P("groups", None), P("groups", None)),
        check_vma=False,
    )
```

```python
import functools

import jax
import jax.numpy as jnp
from jax import lax
from jax.experimental import pallas as pl
from jax.experimental.pallas import tpu as pltpu
from jax.sharding import PartitionSpec as P

R_CELLS = 32
CH = 32
PLANES = 8
LANES = 384
MAIN = 256
PIECES = 14
PIECE = 16
MESH = pl.DeviceIdType.MESH
POSITIONS = [0, 1, 2, 3, 4, 5, 6, 7, -2, -1, 8, 9]
F32 = jnp.float32
BF16 = jnp.bfloat16


def lane_place(position):
    index = POSITIONS.index(position)
    return index // 4, index % 4


HALO = [-2, -1, 8, 9]
INNER = list(range(PLANES))


def kernel(
    n, vertical,
    snap_in, cot_in, w1_in, w2_in, codes_in,
    out_ref, up1_ref, up2_ref,
    snap_ref, cot_ref, w1_ref, w2_ref, codes_ref,
    halo, taps, main1, main2, side1, side2, back1, edge1, edge2,
    xs, xh, xe, cs, ch, ce, hs, hh, ps, ph,
    pg_nat, cot_edge, g1, g2, rs1, rs2, own1, own2, ag1, ag2,
    load_sem, halo_send, halo_recv,
    rs1_send, rs1_recv, rs2_send, rs2_recv, ag1_send, ag1_recv, ag2_send, ag2_recv,
):
    cells = snap_ref.shape[1]
    wide = cells + 2 * vertical
    me = lax.axis_index("blocks")
    after, before = lax.rem(me + 1, n), lax.rem(me + n - 1, n)

    barrier = pltpu.get_barrier_semaphore()

    def greet(k, carry):
        pl.semaphore_signal(
            barrier, inc=1, device_id={"blocks": lax.rem(me + k, n)}, device_id_type=MESH
        )
        return carry

    lax.fori_loop(1, n, greet, 0)

    loads = [
        pltpu.make_async_copy(source, target, load_sem.at[index])
        for index, (source, target) in enumerate([
            (codes_in, codes_ref), (w1_in, w1_ref), (w2_in, w2_ref), (snap_in, snap_ref), (cot_in, cot_ref)
        ])
    ]
    for load in loads:
        load.start()

    for field in (xs, cs, hs, ps):
        field[:, pl.ds(0, vertical), :] = jnp.zeros((3, vertical, MAIN), BF16)
        field[:, pl.ds(wide - vertical, vertical), :] = jnp.zeros((3, vertical, MAIN), BF16)
    for field in (xh, ch, hh, ph, xe, ce):
        field[pl.ds(0, vertical), :] = jnp.zeros((vertical, field.shape[1]), BF16)
        field[pl.ds(wide - vertical, vertical), :] = jnp.zeros((vertical, field.shape[1]), BF16)

    pl.semaphore_wait(barrier, n - 1)

    copies = []
    for index, (source, rows, target, side) in enumerate([
        (snap_in, 6 * CH, after, 0),
        (snap_in, 0, before, 1),
        (cot_in, 6 * CH, after, 0),
        (cot_in, 0, before, 1),
    ]):
        copy = pltpu.make_async_remote_copy(
            src_ref=source.at[pl.ds(rows, 2 * CH)],
            dst_ref=halo.at[side, pl.ds((index // 2) * 2 * CH, 2 * CH)],
            send_sem=halo_send.at[index],
            recv_sem=halo_recv.at[index],
            device_id={"blocks": target},
            device_id_type=MESH,
        )
        copy.start()
        copies.append(copy)

    for load in loads:
        load.wait()

    lane_block = lax.broadcasted_iota(jnp.int32, (CH, 128), 1) // CH
    low, high = codes_ref[0, 0], codes_ref[0, 1]
    code_lane = jnp.where(lane_block < 2, low, high)
    flip_r = (code_lane % 2) == 1
    flip_z = (code_lane // 2) == 1
    spread = (
        lax.broadcasted_iota(jnp.int32, (CH, 128), 0)
        == lax.broadcasted_iota(jnp.int32, (CH, 128), 1) % CH
    ).astype(F32).astype(BF16)

    def tap(da, r, z):
        start = pl.multiple_of((9 * da + 3 * r + z) * CH, CH)
        return taps[pl.ds(start, CH), :]

    def turned(da, r, z):
        return jnp.where(
            flip_r,
            jnp.where(flip_z, tap(da, 2 - r, 2 - z), tap(da, 2 - r, z)),
            jnp.where(flip_z, tap(da, r, 2 - z), tap(da, r, z)),
        )

    def blocks_of(dr):
        made = {}

        def source(da, dz, halo_plane):
            key = (da, dz, halo_plane)
            if key not in made:
                made[key] = turned(da, dr, dz) if halo_plane else tap(da, dr, dz)
            return made[key]

        def block(x, columns):
            parts = tuple(
                (index, x - column[0] + 1, column[1], column[0] in HALO)
                for index, column in enumerate(columns)
                if column is not None and 0 <= x - column[0] + 1 <= 2
            )
            if parts not in made:
                value = jnp.zeros((CH, 128), F32)
                for index, da, dz, halo_plane in parts:
                    value = jnp.where(lane_block == index, source(da, dz, halo_plane), value)
                made[parts] = value.astype(BF16)
            return made[parts]

        return block

    def plane_tiles(dz):
        return [[(y, dz) for y in group] for group in (INNER[:4], INNER[4:], HALO)]

    def spread_taps(weight_ref):
        taps[...] = lax.dot_general(
            weight_ref[...], spread, (((0,), (0,)), ((), ())), preferred_element_type=F32
        )

    def fill(ref, lead, row, tile, value):
        ref[lead, pl.ds(row * CH, CH), pl.ds(tile * 128, 128)] = value

    def build_main(block, dr, main):
        for dz in range(3):
            for row, x in enumerate(INNER):
                for tile in range(2):
                    fill(main, 3 * dr + dz, row, tile, block(x, plane_tiles(dz)[tile]))

    def build_forward(block, dr, side, edge):
        row = 0
        for dz in range(3):
            for x in HALO:
                for tile in range(3):
                    fill(side, dr, row, tile, block(x, plane_tiles(dz)[tile]))
                row += 1
        row = 0
        for dz in range(3):
            for x in (0, 7):
                fill(edge, dr, row, 0, block(x, plane_tiles(dz)[2]))
                row += 1
        for row in (6, 7):
            fill(edge, dr, row, 0, jnp.zeros((CH, 128), BF16))

    def build_backward(block, dr, side, edge, planes):
        for row, x in enumerate(planes):
            for moved in range(3):
                fill(side, dr, row, moved, block(x, plane_tiles(2 - moved)[2]))
        if edge is not None:
            for row, x in enumerate(HALO):
                fill(edge, dr, row, 0, block(x, [(0, 2), (7, 2), (0, 1), (7, 1)]))
                fill(edge, dr, row, 1, block(x, [(0, 0), (7, 0), None, None]))

    def shifts(value):
        rows, lanes = value.shape
        z = lax.broadcasted_iota(jnp.int32, (1, vertical, lanes), 1)

        def moved(steps, outside):
            grid = pltpu.roll(value, steps % rows, 0).reshape(rows // vertical, vertical, lanes)
            return jnp.where(z == outside, 0.0, grid).reshape(rows, lanes)

        return [moved(1, 0), value, moved(-1, vertical - 1)]

    inside = pl.ds(vertical, cells)

    def put_main(dst, value):
        for dz, moved in enumerate(shifts(value)):
            dst[dz, inside, :] = moved.astype(BF16)

    def put_halo(dst, value):
        for dz, moved in enumerate(shifts(value)):
            dst[inside, pl.ds(dz * 128, 128)] = moved.astype(BF16)

    def put_edge(dst, source):
        ends = jnp.concatenate([source[:CH, :], source[7 * CH :, :]] * 2, axis=0)
        moved = shifts(ends.astype(F32).T)
        first = lax.broadcasted_iota(jnp.int32, (cells, 128), 1) < 64
        dst[inside, pl.ds(0, 128)] = jnp.where(first, moved[0], moved[1]).astype(BF16)
        dst[inside, pl.ds(128, 128)] = jnp.where(first, moved[2], 0.0).astype(BF16)

    put_main(xs, snap_ref[...].astype(F32).T)
    put_edge(xe, snap_ref)
    spread_taps(w1_ref)

    def build1(dr, carry):
        block = blocks_of(dr)
        build_main(block, dr, main1)
        build_forward(block, dr, side1, edge1)
        build_backward(block, dr, back1, None, INNER)
        return carry

    lax.fori_loop(0, 3, build1, 0)
    put_main(cs, cot_ref[...].astype(F32).T)
    put_edge(ce, cot_ref)
    cot_edge[pl.ds(0, CH), :] = cot_ref[pl.ds(0, CH), :]
    cot_edge[pl.ds(CH, CH), :] = cot_ref[pl.ds(7 * CH, CH), :]
    spread_taps(w2_ref)

    def build2(dr, carry):
        block = blocks_of(dr)
        build_main(block, dr, main2)
        build_backward(block, dr, side2, edge2, INNER + HALO)
        return carry

    lax.fori_loop(0, 3, build2, 0)

    row_cell = lax.broadcasted_iota(jnp.int32, (cells, cells), 0)
    column_cell = lax.broadcasted_iota(jnp.int32, (cells, cells), 1)
    radial_bits = cells - vertical
    swaps = []
    for code in (low, high):
        mask = (code % 2) * radial_bits + (code // 2) * (vertical - 1)
        swaps.append((row_cell == jnp.bitwise_xor(column_cell, mask)).astype(F32).astype(BF16))

    for copy in copies:
        copy.wait()

    sides = [
        jnp.dot(halo[side], swaps[side], preferred_element_type=F32) for side in range(2)
    ]
    put_halo(xh, jnp.concatenate([sides[0][: 2 * CH], sides[1][: 2 * CH]], axis=0).T)
    put_halo(ch, jnp.concatenate([sides[0][2 * CH :], sides[1][2 * CH :]], axis=0).T)

    def added(total, term):
        return term if total is None else total + term

    def nn(left, right):
        return jnp.dot(left, right, preferred_element_type=F32)

    def nt(left, right):
        return lax.dot_general(left, right, (((1,), (1,)), ((), ())), preferred_element_type=F32)

    def up(step_r):
        return pl.ds(step_r * vertical, cells)

    def forward():
        inner, outer = None, None
        for dr in range(3):
            for dz in range(3):
                inner = added(inner, nn(xs[dz, up(dr), :], main1[3 * dr + dz]))
            inner = added(inner, nn(xh[up(dr), :], side1[dr, :, :MAIN]))
            outer = added(outer, nn(xh[up(dr), :], side1[dr, :, MAIN:]))
            outer = added(outer, nn(xe[up(dr), :], edge1[dr]))
        return inner, outer

    def backward(field, halos, main, side):
        inner = None
        for dr in range(3):
            for dz in range(3):
                inner = added(inner, nt(field[2 - dz, up(2 - dr), :], main[3 * dr + dz]))
            inner = added(inner, nt(halos[up(2 - dr), :], side[dr, :MAIN, :]))
        return inner

    def backward_outer(halos, ends, side, edge):
        outer = None
        for dr in range(3):
            outer = added(outer, nt(halos[up(2 - dr), :], side[dr, MAIN:, :]))
            outer = added(outer, nt(ends[up(2 - dr), :], edge[dr]))
        return outer

    def gradient(left, ends, field, halos, result):
        found = {}
        for dr in range(3):
            outer = nn(ends, halos[up(dr), :])
            for dz in range(3):
                full = nn(left, field[dz, up(dr), :])
                for da in range(3):
                    places = [None] * 4
                    for a in range(PLANES):
                        tile, place = lane_place(a + da - 1)
                        if tile == 2:
                            row = 0 if a == 0 else CH
                            piece = outer[row : row + CH, dz * 128 : (dz + 1) * 128]
                        else:
                            piece = full[a * CH : (a + 1) * CH, tile * 128 : (tile + 1) * 128]
                        places[place] = added(places[place], piece)
                    total = jnp.where(
                        lane_block < 2,
                        jnp.where(lane_block == 0, places[0], places[1]),
                        jnp.where(lane_block == 2, places[2], places[3]),
                    )
                    found[9 * da + 3 * dr + dz] = total
        found[27] = jnp.zeros((CH, 128), F32)
        half = lane_block < 2
        even = lane_block % 2 == 0

        def join(first, second, mask, steps):
            return jnp.where(mask, first, second) + pltpu.roll(
                jnp.where(mask, second, first), steps, 1
            )

        for tile in range(7):
            t0, t1, t2, t3 = (found[4 * tile + place] for place in range(4))
            low_pair, high_pair = join(t0, t2, half, 64), join(t1, t3, half, 64)
            left = jnp.where(even, low_pair, high_pair)
            right_even = pltpu.roll(low_pair, 96, 1)
            right_odd = pltpu.roll(high_pair, 32, 1)
            result[pl.ds(tile * CH, CH), :] = left + jnp.where(even, right_even, right_odd)

    def scatter_copy(grad, slots, send, recv, owner, source):
        return pltpu.make_async_remote_copy(
            src_ref=grad.at[pl.ds(pl.multiple_of(owner * PIECE, PIECE), PIECE)],
            dst_ref=slots.at[source],
            send_sem=send.at[owner],
            recv_sem=recv.at[source],
            device_id={"blocks": owner},
            device_id_type=MESH,
        )

    def scatter_start(grad, slots, send, recv):
        def one(k, carry):
            owner = lax.rem(me + k, n)

            @pl.when(owner < PIECES)
            def _():
                scatter_copy(grad, slots, send, recv, owner, me).start()

            return carry

        lax.fori_loop(1, n, one, 0)

        @pl.when(me < PIECES)
        def _():
            slots[me] = grad[pl.ds(pl.multiple_of(me * PIECE, PIECE), PIECE), :]

    def gather_copy(own, gathered, send, recv, owner, target):
        return pltpu.make_async_remote_copy(
            src_ref=own,
            dst_ref=gathered.at[owner],
            send_sem=send.at[target],
            recv_sem=recv.at[owner],
            device_id={"blocks": target},
            device_id_type=MESH,
        )

    def reduce_and_gather(grad, slots, send, recv, own, gathered, gsend, grecv):
        @pl.when(me < PIECES)
        def _():
            def one(k, carry):
                source = lax.rem(me + k, n)
                scatter_copy(grad, slots, send, recv, me, source).wait_recv()
                return carry

            lax.fori_loop(1, n, one, 0)
            total = jnp.sum(slots[...], axis=0).astype(BF16)
            own[...] = total
            gathered[me] = total

            def out(k, carry):
                gather_copy(own, gathered, gsend, grecv, me, lax.rem(me + k, n)).start()
                return carry

            lax.fori_loop(1, n, out, 0)

    def finish(grad, slots, send, recv, own, gathered, gsend, grecv, up_ref):
        def sent(k, carry):
            owner = lax.rem(me + k, n)

            @pl.when(owner < PIECES)
            def _():
                scatter_copy(grad, slots, send, recv, owner, me).wait_send()
                gather_copy(own, gathered, gsend, grecv, owner, me).wait_recv()

            return carry

        lax.fori_loop(1, n, sent, 0)
        value = gathered[...].astype(F32).reshape(PIECES * PIECE, 128)
        scale = lax.rsqrt(jnp.sum(value * value) / (CH * 27 * CH) + 1e-06)
        value = value * scale
        for tile in range(7):
            lanes = 128 if tile < 6 else 96
            up_ref[:, pl.ds(tile * 128, lanes)] = value[tile * CH : (tile + 1) * CH, :lanes]

        @pl.when(me < PIECES)
        def _():
            def out(k, carry):
                gather_copy(own, gathered, gsend, grecv, me, lax.rem(me + k, n)).wait_send()
                return carry

            lax.fori_loop(1, n, out, 0)

    set1 = (g1, rs1, rs1_send, rs1_recv, own1, ag1, ag1_send, ag1_recv)
    set2 = (g2, rs2, rs2_send, rs2_recv, own2, ag2, ag2_send, ag2_recv)

    def activate(pre):
        s = 1.0 / (1.0 + jnp.exp(-pre))
        return (pre * s).astype(BF16).astype(F32), s * (1.0 + pre * (1.0 - s))

    inner, outer = forward()
    hidden, slope = activate(inner)
    hidden_outer, slope_outer = activate(outer)
    put_main(hs, hidden)
    put_halo(hh, hidden_outer)

    gradient(cot_ref[...], cot_edge[...], hs, hh, g2)
    scatter_start(*set2[:4])

    value = (backward(cs, ch, main2, side2) * slope).astype(BF16).astype(F32)
    put_main(ps, value)
    pg_nat[...] = value.T.astype(BF16)
    value = (backward_outer(ch, ce, side2, edge2) * slope_outer).astype(BF16).astype(F32)
    put_halo(ph, value)

    ends = jnp.concatenate([pg_nat[:CH, :], pg_nat[7 * CH :, :]], axis=0)
    gradient(pg_nat[...], ends, xs, xh, g1)
    scatter_start(*set1[:4])
    reduce_and_gather(*set2)

    out_ref[...] = backward(ps, ph, main1, back1).T + cot_ref[...].astype(F32)

    reduce_and_gather(*set1)
    finish(*set2, up2_ref)
    finish(*set1, up1_ref)


def solution(mesh):
    n = mesh.shape["blocks"]

    def body(snapshot, cotangent, first_weight, second_weight, face_codes):
        cells = snapshot.shape[3]
        vertical = cells // R_CELLS
        wide = cells + 2 * vertical
        flat = (PLANES * CH, cells)
        vmem = pl.BlockSpec(memory_space=pltpu.VMEM)
        dma = pltpu.SemaphoreType.DMA
        grad, up1, up2 = pl.pallas_call(
            functools.partial(kernel, n, vertical),
            out_shape=(
                jax.ShapeDtypeStruct(flat, F32),
                jax.ShapeDtypeStruct(first_weight.shape, F32),
                jax.ShapeDtypeStruct(second_weight.shape, F32),
            ),
            in_specs=[pl.BlockSpec(memory_space=pltpu.HBM)] * 5,
            out_specs=(vmem, vmem, vmem),
            scratch_shapes=[
                pltpu.VMEM(flat, BF16),
                pltpu.VMEM(flat, BF16),
                pltpu.VMEM(first_weight.shape, BF16),
                pltpu.VMEM(second_weight.shape, BF16),
                pltpu.SMEM((1, 2), jnp.int32),
                pltpu.VMEM((2, 4 * CH, cells), BF16),
                pltpu.VMEM((27 * CH, 128), F32),
                pltpu.VMEM((9, MAIN, MAIN), BF16),
                pltpu.VMEM((9, MAIN, MAIN), BF16),
                pltpu.VMEM((3, LANES, LANES), BF16),
                pltpu.VMEM((3, LANES, LANES), BF16),
                pltpu.VMEM((3, MAIN, LANES), BF16),
                pltpu.VMEM((3, MAIN, 128), BF16),
                pltpu.VMEM((3, 128, MAIN), BF16),
                pltpu.VMEM((3, wide, MAIN), BF16),
                pltpu.VMEM((wide, LANES), BF16),
                pltpu.VMEM((wide, MAIN), BF16),
                pltpu.VMEM((3, wide, MAIN), BF16),
                pltpu.VMEM((wide, LANES), BF16),
                pltpu.VMEM((wide, MAIN), BF16),
                pltpu.VMEM((3, wide, MAIN), BF16),
                pltpu.VMEM((wide, LANES), BF16),
                pltpu.VMEM((3, wide, MAIN), BF16),
                pltpu.VMEM((wide, LANES), BF16),
                pltpu.VMEM(flat, BF16),
                pltpu.VMEM((2 * CH, cells), BF16),
                pltpu.VMEM((PIECES * PIECE, 128), F32),
                pltpu.VMEM((PIECES * PIECE, 128), F32),
                pltpu.VMEM((n, PIECE, 128), F32),
                pltpu.VMEM((n, PIECE, 128), F32),
                pltpu.VMEM((PIECE, 128), BF16),
                pltpu.VMEM((PIECE, 128), BF16),
                pltpu.VMEM((PIECES, PIECE, 128), BF16),
                pltpu.VMEM((PIECES, PIECE, 128), BF16),
                dma((5,)),
                dma((4,)),
                dma((4,)),
                dma((PIECES,)),
                dma((n,)),
                dma((PIECES,)),
                dma((n,)),
                dma((n,)),
                dma((PIECES,)),
                dma((n,)),
                dma((PIECES,)),
            ],
            compiler_params=pltpu.CompilerParams(
                collective_id=0, has_side_effects=True, vmem_limit_bytes=63 * 1024 * 1024
            ),
        )(
            snapshot.reshape(flat),
            cotangent.reshape(flat),
            first_weight,
            second_weight,
            face_codes,
        )
        return grad.reshape(snapshot.shape), up1, up2

    return jax.shard_map(
        body,
        mesh=mesh,
        in_specs=(
            P("groups", "blocks", None, None),
            P("groups", "blocks", None, None),
            P(),
            P(),
            P(("groups", "blocks"), None),
        ),
        out_specs=(P("groups", "blocks", None, None), P("groups", None), P("groups", None)),
        check_vma=False,
    )
```
